32 devices in a mesh: tm: 4 (over x, core), freq: 8 (over z, y).
Axes of the slice: x: 2, y: 2, z: 4, core: 2. Of those that a mesh axis runs over, the one named last changes fastest.
Arguments:
- voltages: bfloat16 [4, 1024, 258048], P('tm', 'freq'), may hold values from -6 to 6
- chan_bins: int32 [32], replicated, may hold values from 0 to 2047, as said below
- antenna_map: int32 [1024], replicated, may hold values from 0 to 1023, each once
- beam_index: int32 [512], replicated, may hold values from 0 to 511, each once
- delays: float32 [512, 1024], replicated, may hold values from -4 to 4
Outputs:
- visibilities: float32 [32, 2, 1024, 1024], P(('tm', 'freq'))
- beam_volts: float32 [512, 32, 2, 192], P('freq', 'tm')
The draws below stay inside these ranges and needn't reach their ends.
Inputs may be any that keep to these rules, and one draw needn't show every extreme that they name: `chan_bins`: the 32 bins are distinct, below 2048. `antenna_map`: each signal feeds exactly one antenna input. `beam_index`: each beam has a pointing of its own.
All inputs are finite; a program needn't handle non-finite values.
Results may differ from the reference program's by a relative error of at most 0.006.
Values may be sent and summed in bfloat16 or wider, within the bound.
No kernel may reach another device: no remote copies, remote signals or barrier semaphores. Data moves between devices by JAX's collectives and lax.ppermute only.
A program may use at most 256 MiB of HBM per device.

```python
import math
import jax
import jax.numpy as jnp
from jax import lax

SIG = 1024
NFFT = 4096
TAPS = 16
FR = 48
BEAMS = 512
POINTINGS = 512
TBLOCKS = 4
TIME = 192
CHANNELS = 32


def draw_chan_bins(key, part):
    first_key, second_key = jax.random.split(key)
    half_bins = NFFT // 2
    middle = jax.random.permutation(first_key, half_bins - 2)[:CHANNELS - 2] + 1
    values = jnp.concatenate([jnp.array([0, half_bins - 1], jnp.int32), middle.astype(jnp.int32)])
    ordering = jax.random.permutation(second_key, CHANNELS)
    return values[ordering]


def levels(rng, dims, cuts, smallest, high):
    gain, own = 1.0, jax.random.fold_in(rng, 6)
    for axis_at, blocks in cuts:
        draws = jnp.exp(jax.random.uniform(jax.random.fold_in(own, axis_at), (blocks,), jnp.float32, smallest / len(cuts), high / len(cuts)))
        gain = gain * jnp.repeat(draws, dims[axis_at] // blocks).reshape([-1 if axis == axis_at else 1 for axis in range(len(dims))])
    return gain


def bell_draw(key, dims, scale, limit, shards=(), kind=jnp.bfloat16):
    values = scale * jax.random.normal(key, dims, jnp.float32)
    if shards:
        values = values * levels(key, dims, shards, -0.22, 0.18)
    return jnp.clip(values, -limit, limit).astype(kind)


def setup_inputs(seed: int = 0) -> dict:
    key_list = jax.random.split(jax.random.key(seed), 6)
    voltages = bell_draw(key_list[0], (TBLOCKS, SIG, (FR + TAPS - 1) * NFFT), 1.0, 6.0, ((0, 4), (1, 8)))
    chan_bins = draw_chan_bins(jax.random.fold_in(key_list[5], 71), 0)
    antenna_map = jax.random.permutation(key_list[2], SIG).astype(jnp.int32)
    beam_index = jax.random.permutation(key_list[3], BEAMS).astype(jnp.int32)
    delays = jnp.clip(jax.random.uniform(key_list[4], (POINTINGS, SIG), jnp.float32, -4.0, 4.0), -4.0, 4.0)
    return {"voltages": voltages, "chan_bins": chan_bins, "antenna_map": antenna_map, "beam_index": beam_index, "delays": delays}


def prototype(tap_count, length):
    total = tap_count * length
    offsets = jnp.arange(total, dtype=jnp.float32)
    shifted = (offsets - 0.5 * total + 0.5) / length
    window = 0.5 - 0.5 * jnp.cos(2.0 * math.pi / total * (offsets + 0.5))
    return (jnp.sinc(shifted) * window).reshape(tap_count, length)

def dft_table(bins, length):
    positions = jnp.arange(length, dtype=jnp.int32)
    products = bins[:, None].astype(jnp.int32) * positions[None, :] % length
    angles = products.astype(jnp.float32) * (2.0 * math.pi / length)
    scale = 1.0 / math.sqrt(length)
    return jnp.stack([jnp.cos(angles) * scale, -jnp.sin(angles) * scale]).astype(jnp.bfloat16)

def filter_bank(samples, taps_table, frames):
    total = jnp.zeros((samples.shape[0], frames, samples.shape[2]), jnp.float32)
    for tap_index in range(taps_table.shape[0]):
        total = total + taps_table[tap_index] * samples[:, tap_index:tap_index + frames, :].astype(jnp.float32)
    return total.astype(jnp.bfloat16)

def correlate(volts):
    wide = volts.astype(jnp.float32)
    swapped = jnp.stack([wide[1], -wide[0]])
    real_part = jnp.einsum('rat,rbt->ab', wide, wide)
    imag_part = jnp.einsum('rat,rbt->ab', swapped, wide)
    return jnp.stack([real_part, imag_part]) / volts.shape[2]

def form_beams(volts, selected, bin_value):
    phase = selected * bin_value.astype(jnp.float32) * (2.0 * math.pi / NFFT)
    cosine = jnp.cos(phase).astype(jnp.bfloat16)
    sine = jnp.sin(phase).astype(jnp.bfloat16)
    weights = jnp.stack([jnp.stack([cosine, sine], 1), jnp.stack([-sine, cosine], 1)])
    formed = jnp.einsum('obra,rat->bot', weights.astype(jnp.float32), volts.astype(jnp.float32))
    return formed * (1.0 / math.sqrt(SIG))

def reference(voltages, chan_bins, antenna_map, beam_index, delays):
    taps_table = prototype(TAPS, NFFT)
    table = dft_table(chan_bins, NFFT)
    group = min(SIG, 128)

    def one_group(samples):
        shaped = samples.reshape(group, FR + TAPS - 1, NFFT)
        filtered = filter_bank(shaped, taps_table, FR)
        spectra = jnp.einsum('rcn,gjn->crgj', table.astype(jnp.float32), filtered.astype(jnp.float32))
        return spectra.astype(jnp.bfloat16)

    def one_block(block):
        return lax.map(one_group, block.reshape(SIG // group, group, block.shape[1]))
    spectra = lax.map(one_block, voltages)
    series = spectra.transpose(2, 3, 1, 4, 0, 5).reshape(CHANNELS, 2, SIG, TIME)
    selected = jnp.take(delays, beam_index, axis=0)

    def one_channel(inputs):
        stacked, bin_value = inputs
        volts = jnp.take(stacked, antenna_map, axis=1)
        return (correlate(volts), form_beams(volts, selected, bin_value))
    visibilities, beams = lax.map(one_channel, (series, chan_bins))
    return (visibilities, beams.transpose(1, 0, 2, 3))
```

```python
import functools
import math

import jax
import jax.numpy as jnp
import numpy as np
from jax import lax
from jax.experimental import pallas as pl
from jax.experimental.pallas import tpu as pltpu
from jax.sharding import PartitionSpec as P

NFFT = 4096
TAPS = 16
RANK = 8
LANES = 128
NT = (((1,), (1,)), ((), ()))


def taps_factors():
    total = TAPS * NFFT
    offsets = np.arange(total, dtype=np.float64)
    shifted = (offsets - 0.5 * total + 0.5) / NFFT
    window = 0.5 - 0.5 * np.cos(2.0 * np.pi / total * (offsets + 0.5))
    taps = (np.sinc(shifted) * window).reshape(TAPS, NFFT)
    left, _, _ = np.linalg.svd(taps, full_matrices=False)
    mix = np.round(left[:, :RANK], 7)
    parity = []
    for r in range(RANK):
        sign = 1.0 if np.sum(mix[:, r] * mix[::-1, r]) > 0 else -1.0
        mix[:, r] = 0.5 * (mix[:, r] + sign * mix[::-1, r])
        parity.append(sign)
    gram = np.sum(mix[:, :, None] * mix[:, None, :], axis=0)
    inverse = np.linalg.inv(gram)
    basis = np.zeros((RANK, NFFT))
    for r in range(RANK):
        dual = np.sum(mix * inverse[r], axis=1)
        basis[r] = np.sum(dual[:, None] * taps, axis=0)
    return mix, basis, parity


def term_tiles(parity, per_tile):
    tiles = []
    for wanted in (1.0, -1.0):
        group = [r for r in range(RANK) if parity[r] == wanted]
        for at in range(0, len(group), per_tile):
            tiles.append((tuple(group[at : at + per_tile]), wanted))
    return tiles


def cos_turns(turns):
    rest = 0.25 - jnp.abs(turns - jnp.round(turns))
    angle = rest * (2.0 * math.pi)
    square = angle * angle
    total = -1.0 / math.factorial(11) + square * (1.0 / math.factorial(13))
    for power in (9, 7, 5, 3):
        total = (-1.0) ** (power // 2) / math.factorial(power) + square * total
    return angle + angle * square * total


def spectra_kernel(chunk, chunks_per_step, frames, width, signs,
                   x_ref, w_ref, mix_ref, out_ref, y_ref, acc_ref, turned_ref):
    step = pl.program_id(0)
    signals = x_ref.shape[0]
    columns = w_ref.shape[1]
    lag = (TAPS - 1 + chunk - 1) // chunk + 1
    size = min(width, LANES)
    out_tiles = width // size
    per_tile = LANES // size

    def combine(first, slot):
        for out_tile in range(out_tiles):
            for row in range(0, signals, 8):
                totals = [jnp.zeros((8, LANES), jnp.float32) for _ in range(chunk)]
                for tile in range(out_tile, columns // LANES, out_tiles):
                    held = [
                        y_ref[first + i, row : row + 8, tile * LANES : (tile + 1) * LANES]
                        for i in range(chunk + TAPS - 1)
                    ]
                    for k in range(TAPS // 2):
                        factor = mix_ref[tile, k]
                        for o in range(chunk):
                            low, high = held[o + k], held[o + TAPS - 1 - k]
                            both = low + high if signs[tile // out_tiles] > 0 else low - high
                            totals[o] = totals[o] + factor * both
                for o in range(chunk):
                    acc_ref[o, row : row + 8, :] = totals[o]
            for o in range(chunk):
                turned = acc_ref[o].T
                total = turned[:size]
                for i in range(1, per_tile):
                    total = total + turned[i * size : (i + 1) * size]
                turned_ref[slot * chunk + o, out_tile * size : (out_tile + 1) * size, :] = total

    def one_chunk(inner, carry):
        at = step * chunks_per_step + inner
        combine(jnp.maximum(at - lag, 0) * chunk, at)
        rows = jnp.concatenate(
            [
                x_ref[:, pl.ds(pl.multiple_of((inner * chunk + i) * NFFT, NFFT), NFFT)]
                for i in range(chunk)
            ],
            axis=0,
        )
        product = jnp.dot(rows, w_ref[...], preferred_element_type=jnp.float32)
        y_ref[pl.ds(at * chunk, chunk)] = product.reshape(chunk, signals, columns)
        return carry

    lax.fori_loop(0, chunks_per_step, one_chunk, 0)

    @pl.when(step == pl.num_programs(0) - 1)
    def _():
        chunks = (frames + TAPS - 1) // chunk

        def rest(group, carry):
            combine(group * chunk, group + lag)
            return carry

        lax.fori_loop(chunks - lag, frames // chunk, rest, 0)
        for row in range(width):
            out_ref[row] = turned_ref[pl.ds(lag * chunk, frames), row, :].astype(out_ref.dtype)


def spectra_of(samples, weights, mix, signs, frames):
    signals, length = samples.shape
    in_frames = length // NFFT
    columns = weights.shape[1]
    width = columns // RANK
    chunk = math.gcd(3, math.gcd(in_frames, frames))
    chunks = in_frames // chunk
    per_step = next(d for d in (3, 2, 1) if chunks % d == 0)
    lag = (TAPS - 1 + chunk - 1) // chunk + 1
    body = functools.partial(spectra_kernel, chunk, per_step, frames, width, signs)
    block = per_step * chunk * NFFT
    return pl.pallas_call(
        body,
        grid=(chunks // per_step,),
        in_specs=[
            pl.BlockSpec((signals, block), lambda i: (0, i)),
            pl.BlockSpec(weights.shape, lambda i: (0, 0), pipeline_mode=pl.Buffered(1)),
            pl.BlockSpec(mix.shape, lambda i: (0, 0, 0, 0), pipeline_mode=pl.Buffered(1)),
        ],
        out_specs=pl.BlockSpec((width, frames, signals), lambda i: (0, 0, 0)),
        out_shape=jax.ShapeDtypeStruct((width, frames, signals), jnp.bfloat16),
        scratch_shapes=[
            pltpu.VMEM((in_frames, signals, columns), jnp.float32),
            pltpu.VMEM((chunk, signals, LANES), jnp.float32),
            pltpu.VMEM((frames + lag * chunk, width, signals), jnp.float32),
        ],
        compiler_params=pltpu.CompilerParams(vmem_limit_bytes=60 << 20),
        cost_estimate=pl.CostEstimate(
            flops=2 * signals * length * columns,
            bytes_accessed=2 * signals * length,
            transcendentals=0,
        ),
        name="spectra",
    )(samples, weights, mix)


def steering_kernel(bin_ref, delays_ref, beams_ref, antennas_ref, table_ref, place_ref, raw_ref):
    pointings, antennas = delays_ref.shape
    beams = beams_ref.shape[1]
    rows = 32
    turn = bin_ref[0, 0]

    def some(at, carry):
        window = pl.ds(pl.multiple_of(at * rows, rows), rows)
        turns = delays_ref[window, :] * turn * (1.0 / NFFT)
        raw_ref[window, :antennas] = cos_turns(turns).astype(jnp.bfloat16)
        raw_ref[window, antennas:] = cos_turns(turns - 0.25).astype(jnp.bfloat16)
        return carry

    lax.fori_loop(0, pointings // rows, some, 0)
    column = jnp.broadcast_to(antennas_ref[...], (LANES, antennas)).T
    for tile in range(antennas // LANES):
        lanes = lax.broadcasted_iota(jnp.int32, (antennas, LANES), 1) + tile * LANES
        place_ref[:, tile * LANES : (tile + 1) * LANES] = jnp.where(
            column == lanes, 1.0, 0.0
        ).astype(jnp.bfloat16)
    wanted = jnp.broadcast_to(beams_ref[...], (LANES, beams)).T
    chosen = jnp.concatenate(
        [
            jnp.where(
                wanted == lax.broadcasted_iota(jnp.int32, (beams, LANES), 1) + tile * LANES, 1.0, 0.0
            ).astype(jnp.bfloat16)
            for tile in range(pointings // LANES)
        ],
        axis=1,
    )
    for part in range(2):
        ordered = jnp.dot(
            chosen, raw_ref[:, part * antennas : (part + 1) * antennas],
            preferred_element_type=jnp.float32,
        ).astype(jnp.bfloat16)
        table_ref[part] = jnp.dot(
            ordered, place_ref[...], preferred_element_type=jnp.float32
        ).astype(jnp.bfloat16)


def steering_of(bin_value, delays, beam_index, antenna_map):
    pointings, antennas = delays.shape
    beams = beam_index.shape[0]
    vmem = pl.BlockSpec(memory_space=pltpu.VMEM)
    return pl.pallas_call(
        steering_kernel,
        in_specs=[pl.BlockSpec(memory_space=pltpu.SMEM), vmem, vmem, vmem],
        out_specs=[vmem, vmem],
        out_shape=[
            jax.ShapeDtypeStruct((2, beams, antennas), jnp.bfloat16),
            jax.ShapeDtypeStruct((antennas, antennas), jnp.bfloat16),
        ],
        scratch_shapes=[pltpu.VMEM((pointings, 2 * antennas), jnp.bfloat16)],
        compiler_params=pltpu.CompilerParams(vmem_limit_bytes=32 << 20),
        cost_estimate=pl.CostEstimate(
            flops=40 * pointings * antennas + 4 * beams * antennas * (antennas + pointings),
            bytes_accessed=8 * pointings * antennas,
            transcendentals=0,
        ),
        name="steering",
    )(bin_value.reshape(1, 1), delays, beam_index.reshape(1, beams), antenna_map.reshape(1, antennas))


def series_of(moved):
    if len(moved.shape) == 3:
        real, imag = moved[0], moved[1]
    else:
        blocks, groups = moved.shape[:2]
        real, imag = (
            jnp.concatenate(
                [
                    jnp.concatenate([moved[q, f, part] for f in range(groups)], axis=1)
                    for q in range(blocks)
                ],
                axis=0,
            )
            for part in range(2)
        )
    return jnp.concatenate([real, imag], axis=0), jnp.concatenate([imag, -real], axis=0)


def beams_kernel(scale, moved_ref, table_ref, out_ref):
    straight, crossed = series_of(moved_ref)
    formed = lax.dot_general(table_ref[0], straight, NT, preferred_element_type=jnp.float32)
    formed += lax.dot_general(table_ref[1], crossed, NT, preferred_element_type=jnp.float32)
    formed = (formed * scale).astype(out_ref.dtype)
    out_ref[...] = formed.reshape(out_ref.shape)


def beams_of(moved, table, groups, times):
    _, beams, antennas = table.shape
    vmem = pl.BlockSpec(memory_space=pltpu.VMEM)
    return pl.pallas_call(
        functools.partial(beams_kernel, 1.0 / math.sqrt(antennas)),
        in_specs=[vmem, vmem],
        out_specs=vmem,
        out_shape=jax.ShapeDtypeStruct((groups, beams // groups, 2 * times), jnp.bfloat16),
        compiler_params=pltpu.CompilerParams(vmem_limit_bytes=32 << 20),
        name="beams",
    )(moved, table)


def visibility_kernel(moved_ref, place_ref, out_ref, straight_ref, crossed_ref):
    step = pl.program_id(0)
    rows = out_ref.shape[2]
    times = straight_ref.shape[1] // 2

    @pl.when(step == 0)
    def _():
        for wide, held in zip(series_of(moved_ref), (straight_ref, crossed_ref)):
            held[...] = lax.dot_general(
                place_ref[...], wide, NT, preferred_element_type=jnp.float32
            ).astype(jnp.bfloat16)

    window = pl.ds(pl.multiple_of(step * rows, rows), rows)
    for part, held in enumerate((straight_ref, crossed_ref)):
        out_ref[0, part] = lax.dot_general(
            held[window, :], straight_ref[...], NT, preferred_element_type=jnp.float32
        ) * (1.0 / times)


def visibilities_of(moved, place, times):
    antennas = place.shape[0]
    rows = antennas // 4
    return pl.pallas_call(
        visibility_kernel,
        grid=(antennas // rows,),
        in_specs=[
            pl.BlockSpec(moved.shape, lambda i: (0,) * len(moved.shape)),
            pl.BlockSpec(place.shape, lambda i: (0, 0)),
        ],
        out_specs=pl.BlockSpec((1, 2, rows, antennas), lambda i: (0, 0, i, 0)),
        out_shape=jax.ShapeDtypeStruct((1, 2, antennas, antennas), jnp.float32),
        scratch_shapes=[pltpu.VMEM((antennas, 2 * times), jnp.bfloat16)] * 2,
        compiler_params=pltpu.CompilerParams(vmem_limit_bytes=32 << 20),
        cost_estimate=pl.CostEstimate(
            flops=8 * antennas * antennas * 2 * times,
            bytes_accessed=8 * antennas * antennas,
            transcendentals=0,
        ),
        name="visibilities",
    )(moved, place)


def body(voltages, chan_bins, antenna_map, beam_index, delays):
    signals_dev = voltages.shape[1]
    frames = voltages.shape[2] // NFFT - TAPS + 1
    channels = chan_bins.shape[0]
    tm_count = lax.axis_size("tm")
    freq_count = lax.axis_size("freq")
    times = tm_count * frames

    mix, basis, parity = taps_factors()
    per_tile = max(1, LANES // (2 * channels))
    tiles = term_tiles(parity, per_tile)
    order = [r for terms, _ in tiles for r in terms]
    signs = tuple(sign for _, sign in tiles)
    lanes = np.repeat(mix[: TAPS // 2, order], 2 * channels, axis=1).astype(np.float32)
    lanes = lanes.reshape(TAPS // 2, -1, 1, LANES).transpose(1, 0, 2, 3)
    mix_lanes = jnp.broadcast_to(jnp.asarray(lanes), (lanes.shape[0], TAPS // 2, 8, LANES))

    positions = jnp.arange(NFFT, dtype=jnp.int32)
    products = positions[:, None] * jnp.repeat(chan_bins, 2)[None, :] % NFFT
    quarter = jnp.asarray(np.tile(np.array([0.0, 0.25], np.float32), channels))
    table = cos_turns(products.astype(jnp.float32) * (1.0 / NFFT) + quarter)
    table = (table * (1.0 / math.sqrt(NFFT))).astype(jnp.bfloat16).astype(jnp.float32)
    basis_columns = jnp.asarray(basis[order].T.astype(np.float32))
    weights = (basis_columns[:, :, None] * table[:, None, :]).astype(jnp.bfloat16)
    weights = weights.reshape(NFFT, RANK * 2 * channels)

    spectra = spectra_of(voltages[0], weights, mix_lanes, signs, frames)
    spectra = spectra.reshape(channels, 2, frames, signals_dev)
    moved = lax.all_to_all(spectra, ("tm", "freq"), split_axis=0, concat_axis=0, tiled=True)
    moved = moved.reshape(tm_count, freq_count, 2, frames, signals_dev)
    if signals_dev % LANES:
        moved = moved.transpose(2, 0, 3, 1, 4).reshape(2, times, freq_count * signals_dev)

    channel = lax.axis_index("tm") * freq_count + lax.axis_index("freq")
    bin_value = lax.dynamic_index_in_dim(chan_bins, channel, keepdims=False)
    table, place = steering_of(bin_value.astype(jnp.float32), delays, beam_index, antenna_map)
    formed = beams_of(moved, table, freq_count, times)
    turned = lax.all_to_all(formed, "freq", split_axis=0, concat_axis=0, tiled=True)
    visibilities = visibilities_of(moved, place, times)
    turned = turned.transpose(1, 0, 2).astype(jnp.float32)
    return (visibilities, turned.reshape(turned.shape[0], turned.shape[1], 2, times))


def solution(mesh):
    return jax.shard_map(
        body,
        mesh=mesh,
        in_specs=(P("tm", "freq", None), P(), P(), P(), P()),
        out_specs=(P(("tm", "freq"), None, None, None), P("freq", "tm", None, None)),
        check_vma=False,
    )
```

```python
import functools
import math

import jax
import jax.numpy as jnp
import numpy as np
from jax import lax
from jax.experimental import pallas as pl
from jax.experimental.pallas import tpu as pltpu
from jax.sharding import PartitionSpec as P

NFFT = 4096
TAPS = 16
RANK = 8
LANES = 128
NT = (((1,), (1,)), ((), ()))


def taps_factors():
    total = TAPS * NFFT
    offsets = np.arange(total, dtype=np.float64)
    shifted = (offsets - 0.5 * total + 0.5) / NFFT
    window = 0.5 - 0.5 * np.cos(2.0 * np.pi / total * (offsets + 0.5))
    taps = (np.sinc(shifted) * window).reshape(TAPS, NFFT)
    left, _, _ = np.linalg.svd(taps, full_matrices=False)
    mix = np.round(left[:, :RANK], 7)
    parity = []
    for r in range(RANK):
        sign = 1.0 if np.sum(mix[:, r] * mix[::-1, r]) > 0 else -1.0
        mix[:, r] = 0.5 * (mix[:, r] + sign * mix[::-1, r])
        parity.append(sign)
    gram = np.sum(mix[:, :, None] * mix[:, None, :], axis=0)
    inverse = np.linalg.inv(gram)
    basis = np.zeros((RANK, NFFT))
    for r in range(RANK):
        dual = np.sum(mix * inverse[r], axis=1)
        basis[r] = np.sum(dual[:, None] * taps, axis=0)
    return mix, basis, parity


def term_tiles(parity, per_tile):
    tiles = []
    for half in (range(RANK // 2), range(RANK // 2, RANK)):
        for wanted in (1.0, -1.0):
            group = [r for r in half if parity[r] == wanted]
            for at in range(0, len(group), per_tile):
                tiles.append((tuple(group[at : at + per_tile]), wanted))
    return tiles


def cos_turns(turns):
    rest = 0.25 - jnp.abs(turns - jnp.round(turns))
    angle = rest * (2.0 * math.pi)
    square = angle * angle
    total = -1.0 / math.factorial(11) + square * (1.0 / math.factorial(13))
    for power in (9, 7, 5, 3):
        total = (-1.0) ** (power // 2) / math.factorial(power) + square * total
    return angle + angle * square * total


def fill_weights(bins_ref, basis_ref, w_ref, width, out_tiles):
    columns = w_ref.shape[1]
    splits = basis_ref.shape[1]
    block = 2 * LANES
    half = NFFT // 2
    source = lax.broadcasted_iota(jnp.int32, (splits, columns), 0)
    term = lax.broadcasted_iota(jnp.int32, (splits, columns), 1) // width
    spread = jnp.where(source % RANK == term, 1.0, 0.0).astype(jnp.bfloat16)
    lane = lax.broadcasted_iota(jnp.int32, (1, LANES), 1)
    quarter = jnp.where(lane % 2 == 1, 0.25, 0.0)
    lane_bins = []
    for out_tile in range(out_tiles):
        channel = (lane + out_tile * LANES) % width // 2
        value = jnp.zeros((1, LANES), jnp.int32)
        for at in range(width // 2):
            value = jnp.where(channel == at, bins_ref[at], value)
        lane_bins.append(value)

    def some(at, carry):
        windows = [pl.ds(pl.multiple_of(at * block + i * half, block), block) for i in range(2)]
        rows = lax.broadcasted_iota(jnp.int32, (block, LANES), 0) + at * block
        factors = [
            jnp.dot(basis_ref[window, :], spread, preferred_element_type=jnp.float32)
            for window in windows
        ]
        for out_tile, bins in enumerate(lane_bins):
            turns = rows.astype(jnp.float32) * (bins.astype(jnp.float32) * (1.0 / NFFT))
            turns = turns - jnp.round(turns)
            table = cos_turns(turns + quarter) * (1.0 / math.sqrt(NFFT))
            table = table.astype(jnp.bfloat16).astype(jnp.float32)
            flipped = table * jnp.where(bins % 2 == 1, -1.0, 1.0)
            for tile in range(out_tile, columns // LANES, out_tiles):
                lanes = slice(tile * LANES, (tile + 1) * LANES)
                for window, values, factor in zip(windows, (table, flipped), factors):
                    w_ref[window, lanes] = (values * factor[:, lanes]).astype(w_ref.dtype)
        return carry

    lax.fori_loop(0, half // block, some, 0)


def spectra_kernel(chunk, frames, width, signs,
                   bins_ref, basis_ref, mix_ref, minor_mix_ref, x_ref, out_ref,
                   w_ref, major_ref, minor_ref, acc_ref, turned_ref):
    step = pl.program_id(0)
    signals = x_ref.shape[0]
    columns = w_ref.shape[1]
    behind = TAPS - 1 + chunk
    pad = behind % chunk
    size = min(width, LANES)
    out_tiles = width // size

    @pl.when(step == 0)
    def _():
        fill_weights(bins_ref, basis_ref, w_ref, width, out_tiles)
        major_ref[: behind + pad] = jnp.zeros((behind + pad,) + major_ref.shape[1:], jnp.float32)
        minor_ref[: behind + pad] = jnp.zeros((behind + pad,) + minor_ref.shape[1:], jnp.bfloat16)

    def weigh(totals, held, factors, sign):
        for k in range(TAPS // 2):
            for o in range(chunk):
                low, high = held[o + k], held[o + TAPS - 1 - k]
                totals[o] = totals[o] + factors[k] * (low + high if sign > 0 else low - high)

    def combine(slot, start):
        first = jnp.maximum(slot * chunk - behind + pad, 0)
        seen = None
        for out_tile in range(out_tiles):
            small = [jnp.zeros((16, LANES), jnp.bfloat16) for _ in range(chunk)]
            for tile in range(out_tile, columns // 2 // LANES, out_tiles):
                lanes = slice(tile * LANES, (tile + 1) * LANES)
                held = [minor_ref[first + i, pl.ds(start, 16), lanes] for i in range(chunk + TAPS - 1)]
                factors = [minor_mix_ref[tile, k] for k in range(TAPS // 2)]
                weigh(small, held, factors, signs[(columns // 2 // LANES + tile) // out_tiles])
            wide = [total.astype(jnp.float32) for total in small]
            for row in (0, 8):
                window = pl.ds(start + row, 8)
                totals = [total[row : row + 8] for total in wide]
                for tile in range(out_tile, columns // 2 // LANES, out_tiles):
                    lanes = slice(tile * LANES, (tile + 1) * LANES)
                    held = [major_ref[first + i, window, lanes] for i in range(chunk + TAPS - 1)]
                    factors = [mix_ref[tile, k : k + 1, :] for k in range(TAPS // 2)]
                    weigh(totals, held, factors, signs[tile // out_tiles])
                for o in range(chunk):
                    acc_ref[slot * chunk + o, out_tile, window, :] = totals[o]
                    seen = totals[o] if seen is None else seen + totals[o]
        return jnp.maximum(jnp.minimum(seen, 0.0), 0.0)

    def turn(slot):
        unit = jnp.where(
            lax.broadcasted_iota(jnp.int32, (size, 2 * LANES), 0)
            == lax.broadcasted_iota(jnp.int32, (size, 2 * LANES), 1) % size, 1.0, 0.0
        ).astype(jnp.bfloat16)
        together = chunk if signals % LANES == 0 else 1
        for out_tile in range(out_tiles):
            for at in range(0, chunk, together):
                total = jnp.concatenate(
                    [acc_ref[slot * chunk + at + i, out_tile] for i in range(together)], axis=0
                )
                high = total.astype(jnp.bfloat16)
                low = (total - high.astype(jnp.float32)).astype(jnp.bfloat16)
                both = jnp.concatenate([high, low], axis=1)
                turned = lax.dot_general(unit, both, NT, preferred_element_type=jnp.float32)
                for i in range(together):
                    turned_ref[out_tile * size : (out_tile + 1) * size, slot * chunk + at + i, :] = (
                        turned[:, i * signals : (i + 1) * signals]
                    )

    turn(jnp.maximum(step - 1, 0))
    pieces = 16
    depth = NFFT // pieces
    zero = product = None
    for piece in range(pieces):
        parts = [x_ref[:, i * NFFT + piece * depth : i * NFFT + (piece + 1) * depth] for i in range(chunk)]
        if zero is not None:
            zero = jnp.concatenate([zero, zero], axis=0).astype(jnp.bfloat16)
            top = jnp.concatenate([parts[0][:16, :LANES] + zero, parts[0][:16, LANES:]], axis=1)
            parts[0] = jnp.concatenate([top, parts[0][16:]], axis=0)
        part = jnp.dot(
            jnp.concatenate(parts, axis=0),
            w_ref[piece * depth : (piece + 1) * depth, :],
            preferred_element_type=jnp.float32,
        )
        product = part if product is None else product + part
        zero = None
        for start in range(piece * 16, signals, pieces * 16):
            zero = combine(step, start)
    window = pl.ds(step * chunk + pad, chunk)
    major_ref[window] = product[:, : columns // 2].reshape(chunk, signals, columns // 2)
    minor = product[:, columns // 2 :].astype(jnp.bfloat16)
    minor_ref[window] = minor.reshape(chunk, signals, columns // 2)

    @pl.when(step == pl.num_programs(0) - 1)
    def _():
        chunks = (frames + TAPS - 1) // chunk
        for start in range(0, signals, 16):
            combine(chunks, start)
        turn(chunks - 1)
        turn(chunks)
        for row in range(width):
            out_ref[row] = turned_ref[row, behind : behind + frames, :].astype(out_ref.dtype)


def spectra_of(samples, chan_bins, frames):
    signals, length = samples.shape
    in_frames = length // NFFT
    width = 2 * chan_bins.shape[0]
    columns = RANK * width
    size = min(width, LANES)
    out_tiles = width // size
    chunk = max(d for d in (1, 2, 3) if in_frames % d == 0)
    behind = TAPS - 1 + chunk
    slots = (in_frames // chunk + 1) * chunk

    mix, basis, parity = taps_factors()
    tiles = term_tiles(parity, LANES // size)
    signs = tuple(sign for _, sign in tiles)
    order = [r for terms, _ in tiles for r in terms]
    lanes = np.repeat(mix[: TAPS // 2, order], width, axis=1).astype(np.float32)
    lanes = lanes.reshape(TAPS // 2, -1, LANES).transpose(1, 0, 2)
    major, minor = np.split(lanes, 2)
    minor = np.repeat(minor[:, :, None, :], 16, axis=2).astype(jnp.bfloat16)
    pieces, left = [], basis[order].T.astype(np.float32)
    for _ in range(3):
        pieces.append(left.astype(jnp.bfloat16))
        left = left - pieces[-1].astype(np.float32)
    pieces.append(np.zeros((NFFT, LANES - 3 * RANK), jnp.bfloat16))

    whole = pl.BlockSpec(memory_space=pltpu.VMEM)
    return pl.pallas_call(
        functools.partial(spectra_kernel, chunk, frames, width, signs),
        grid=(in_frames // chunk,),
        in_specs=[
            pl.BlockSpec(memory_space=pltpu.SMEM), whole, whole, whole,
            pl.BlockSpec((signals, chunk * NFFT), lambda i: (0, i)),
        ],
        out_specs=pl.BlockSpec((width, frames, signals), lambda i: (0, 0, 0)),
        out_shape=jax.ShapeDtypeStruct((width, frames, signals), jnp.bfloat16),
        scratch_shapes=[
            pltpu.VMEM((NFFT, columns), jnp.bfloat16),
            pltpu.VMEM((in_frames + behind % chunk, signals, columns // 2), jnp.float32),
            pltpu.VMEM((in_frames + behind % chunk, signals, columns // 2), jnp.bfloat16),
            pltpu.VMEM((slots, out_tiles, signals, LANES), jnp.float32),
            pltpu.VMEM((width, slots, signals), jnp.float32),
        ],
        compiler_params=pltpu.CompilerParams(vmem_limit_bytes=60 << 20),
        cost_estimate=pl.CostEstimate(
            flops=2 * signals * length * columns,
            bytes_accessed=2 * signals * length,
            transcendentals=0,
        ),
        name="spectra",
    )(chan_bins, jnp.asarray(np.concatenate(pieces, axis=1)), jnp.asarray(major), jnp.asarray(minor), samples)


def steering_kernel(bin_ref, delays_ref, beams_ref, antennas_ref, table_ref, place_ref, raw_ref):
    pointings, antennas = delays_ref.shape
    beams = beams_ref.shape[1]
    rows = 32
    turn = bin_ref[0, 0]

    def some(at, carry):
        window = pl.ds(pl.multiple_of(at * rows, rows), rows)
        turns = delays_ref[window, :] * turn * (1.0 / NFFT)
        raw_ref[window, :antennas] = cos_turns(turns).astype(jnp.bfloat16)
        raw_ref[window, antennas:] = cos_turns(turns - 0.25).astype(jnp.bfloat16)
        return carry

    lax.fori_loop(0, pointings // rows, some, 0)
    column = jnp.broadcast_to(antennas_ref[...], (LANES, antennas)).T
    for tile in range(antennas // LANES):
        lanes = lax.broadcasted_iota(jnp.int32, (antennas, LANES), 1) + tile * LANES
        place_ref[:, tile * LANES : (tile + 1) * LANES] = jnp.where(
            column == lanes, 1.0, 0.0
        ).astype(jnp.bfloat16)
    wanted = jnp.broadcast_to(beams_ref[...], (LANES, beams)).T
    chosen = jnp.concatenate(
        [
            jnp.where(
                wanted == lax.broadcasted_iota(jnp.int32, (beams, LANES), 1) + tile * LANES, 1.0, 0.0
            ).astype(jnp.bfloat16)
            for tile in range(pointings // LANES)
        ],
        axis=1,
    )
    for part in range(2):
        ordered = jnp.dot(
            chosen, raw_ref[:, part * antennas : (part + 1) * antennas],
            preferred_element_type=jnp.float32,
        ).astype(jnp.bfloat16)
        table_ref[part] = jnp.dot(
            ordered, place_ref[...], preferred_element_type=jnp.float32
        ).astype(jnp.bfloat16)


def steering_of(bin_value, delays, beam_index, antenna_map):
    pointings, antennas = delays.shape
    beams = beam_index.shape[0]
    vmem = pl.BlockSpec(memory_space=pltpu.VMEM)
    return pl.pallas_call(
        steering_kernel,
        in_specs=[pl.BlockSpec(memory_space=pltpu.SMEM), vmem, vmem, vmem],
        out_specs=[vmem, vmem],
        out_shape=[
            jax.ShapeDtypeStruct((2, beams, antennas), jnp.bfloat16),
            jax.ShapeDtypeStruct((antennas, antennas), jnp.bfloat16),
        ],
        scratch_shapes=[pltpu.VMEM((pointings, 2 * antennas), jnp.bfloat16)],
        compiler_params=pltpu.CompilerParams(vmem_limit_bytes=32 << 20),
        cost_estimate=pl.CostEstimate(
            flops=40 * pointings * antennas + 4 * beams * antennas * (antennas + pointings),
            bytes_accessed=8 * pointings * antennas,
            transcendentals=0,
        ),
        name="steering",
    )(bin_value.reshape(1, 1), delays, beam_index.reshape(1, beams), antenna_map.reshape(1, antennas))


def series_of(moved):
    if len(moved.shape) == 3:
        real, imag = moved[0], moved[1]
    else:
        blocks, groups = moved.shape[:2]
        real, imag = (
            jnp.concatenate(
                [
                    jnp.concatenate([moved[q, f, part] for f in range(groups)], axis=1)
                    for q in range(blocks)
                ],
                axis=0,
            )
            for part in range(2)
        )
    return jnp.concatenate([real, imag], axis=0), jnp.concatenate([imag, -real], axis=0)


def beams_kernel(scale, moved_ref, table_ref, out_ref):
    straight, crossed = series_of(moved_ref)
    formed = lax.dot_general(table_ref[0], straight, NT, preferred_element_type=jnp.float32)
    formed += lax.dot_general(table_ref[1], crossed, NT, preferred_element_type=jnp.float32)
    formed = (formed * scale).astype(out_ref.dtype)
    out_ref[...] = formed.reshape(out_ref.shape)


def beams_of(moved, table, groups, times):
    _, beams, antennas = table.shape
    vmem = pl.BlockSpec(memory_space=pltpu.VMEM)
    return pl.pallas_call(
        functools.partial(beams_kernel, 1.0 / math.sqrt(antennas)),
        in_specs=[vmem, vmem],
        out_specs=vmem,
        out_shape=jax.ShapeDtypeStruct((groups, beams // groups, 2 * times), jnp.bfloat16),
        compiler_params=pltpu.CompilerParams(vmem_limit_bytes=32 << 20),
        name="beams",
    )(moved, table)


def visibility_kernel(moved_ref, place_ref, out_ref, straight_ref, crossed_ref):
    step = pl.program_id(0)
    rows = out_ref.shape[2]
    times = straight_ref.shape[1] // 2

    @pl.when(step == 0)
    def _():
        for wide, held in zip(series_of(moved_ref), (straight_ref, crossed_ref)):
            held[...] = lax.dot_general(
                place_ref[...], wide, NT, preferred_element_type=jnp.float32
            ).astype(jnp.bfloat16)

    window = pl.ds(pl.multiple_of(step * rows, rows), rows)
    for part, held in enumerate((straight_ref, crossed_ref)):
        out_ref[0, part] = lax.dot_general(
            held[window, :], straight_ref[...], NT, preferred_element_type=jnp.float32
        ) * (1.0 / times)


def visibilities_of(moved, place, times):
    antennas = place.shape[0]
    rows = antennas // 4
    return pl.pallas_call(
        visibility_kernel,
        grid=(antennas // rows,),
        in_specs=[
            pl.BlockSpec(moved.shape, lambda i: (0,) * len(moved.shape)),
            pl.BlockSpec(place.shape, lambda i: (0, 0)),
        ],
        out_specs=pl.BlockSpec((1, 2, rows, antennas), lambda i: (0, 0, i, 0)),
        out_shape=jax.ShapeDtypeStruct((1, 2, antennas, antennas), jnp.float32),
        scratch_shapes=[pltpu.VMEM((antennas, 2 * times), jnp.bfloat16)] * 2,
        compiler_params=pltpu.CompilerParams(vmem_limit_bytes=32 << 20),
        cost_estimate=pl.CostEstimate(
            flops=8 * antennas * antennas * 2 * times,
            bytes_accessed=8 * antennas * antennas,
            transcendentals=0,
        ),
        name="visibilities",
    )(moved, place)


def body(voltages, chan_bins, antenna_map, beam_index, delays):
    signals_dev = voltages.shape[1]
    frames = voltages.shape[2] // NFFT - TAPS + 1
    channels = chan_bins.shape[0]
    tm_count = lax.axis_size("tm")
    freq_count = lax.axis_size("freq")
    times = tm_count * frames

    spectra = spectra_of(voltages[0], chan_bins, frames)
    spectra = spectra.reshape(channels, 2, frames, signals_dev)
    moved = lax.all_to_all(spectra, ("tm", "freq"), split_axis=0, concat_axis=0, tiled=True)
    moved = moved.reshape(tm_count, freq_count, 2, frames, signals_dev)
    if signals_dev % LANES:
        moved = moved.transpose(2, 0, 3, 1, 4).reshape(2, times, freq_count * signals_dev)

    channel = lax.axis_index("tm") * freq_count + lax.axis_index("freq")
    bin_value = lax.dynamic_index_in_dim(chan_bins, channel, keepdims=False)
    table, place = steering_of(bin_value.astype(jnp.float32), delays, beam_index, antenna_map)
    formed = beams_of(moved, table, freq_count, times)
    turned = lax.all_to_all(formed, "freq", split_axis=0, concat_axis=0, tiled=True)
    visibilities = visibilities_of(moved, place, times)
    turned = turned.transpose(1, 0, 2).astype(jnp.float32)
    return (visibilities, turned.reshape(turned.shape[0], turned.shape[1], 2, times))


def solution(mesh):
    return jax.shard_map(
        body,
        mesh=mesh,
        in_specs=(P("tm", "freq", None), P(), P(), P(), P()),
        out_specs=(P(("tm", "freq"), None, None, None), P("freq", "tm", None, None)),
        check_vma=False,
    )
```

```python
import functools
import math

import jax
import jax.numpy as jnp
import numpy as np
from jax import lax
from jax.experimental import pallas as pl
from jax.experimental.pallas import tpu as pltpu
from jax.sharding import PartitionSpec as P

NFFT = 4096
TAPS = 16
RANK = 8
LANES = 128
NT = (((1,), (1,)), ((), ()))


def taps_factors():
    total = TAPS * NFFT
    offsets = np.arange(total, dtype=np.float64)
    shifted = (offsets - 0.5 * total + 0.5) / NFFT
    window = 0.5 - 0.5 * np.cos(2.0 * np.pi / total * (offsets + 0.5))
    taps = (np.sinc(shifted) * window).reshape(TAPS, NFFT)
    left, _, _ = np.linalg.svd(taps, full_matrices=False)
    mix = np.round(left[:, :RANK], 7)
    parity = []
    for r in range(RANK):
        sign = 1.0 if np.sum(mix[:, r] * mix[::-1, r]) > 0 else -1.0
        mix[:, r] = 0.5 * (mix[:, r] + sign * mix[::-1, r])
        parity.append(sign)
    gram = np.sum(mix[:, :, None] * mix[:, None, :], axis=0)
    inverse = np.linalg.inv(gram)
    basis = np.zeros((RANK, NFFT))
    for r in range(RANK):
        dual = np.sum(mix * inverse[r], axis=1)
        basis[r] = np.sum(dual[:, None] * taps, axis=0)
    return mix, basis, parity


def term_tiles(parity, per_tile):
    tiles = []
    for half in (range(RANK // 2), range(RANK // 2, RANK)):
        for wanted in (1.0, -1.0):
            group = [r for r in half if parity[r] == wanted]
            for at in range(0, len(group), per_tile):
                tiles.append((tuple(group[at : at + per_tile]), wanted))
    return tiles


def cos_turns(turns):
    rest = 0.25 - jnp.abs(turns - jnp.round(turns))
    angle = rest * (2.0 * math.pi)
    square = angle * angle
    total = -1.0 / math.factorial(11) + square * (1.0 / math.factorial(13))
    for power in (9, 7, 5, 3):
        total = (-1.0) ** (power // 2) / math.factorial(power) + square * total
    return angle + angle * square * total


def fill_weights(bins_ref, basis_ref, w_ref, width, out_tiles):
    columns = w_ref.shape[1]
    splits = basis_ref.shape[1]
    block = 2 * LANES
    half = NFFT // 2
    source = lax.broadcasted_iota(jnp.int32, (splits, columns), 0)
    term = lax.broadcasted_iota(jnp.int32, (splits, columns), 1) // width
    spread = jnp.where(source % RANK == term, 1.0, 0.0).astype(jnp.bfloat16)
    lane = lax.broadcasted_iota(jnp.int32, (1, LANES), 1)
    quarter = jnp.where(lane % 2 == 1, 0.25, 0.0)
    lane_bins = []
    for out_tile in range(out_tiles):
        channel = (lane + out_tile * LANES) % width // 2
        value = jnp.zeros((1, LANES), jnp.int32)
        for at in range(width // 2):
            value = jnp.where(channel == at, bins_ref[at], value)
        lane_bins.append(value)

    def some(at, carry):
        windows = [pl.ds(pl.multiple_of(at * block + i * half, block), block) for i in range(2)]
        rows = lax.broadcasted_iota(jnp.int32, (block, LANES), 0) + at * block
        factors = [
            jnp.dot(basis_ref[window, :], spread, preferred_element_type=jnp.float32)
            for window in windows
        ]
        for out_tile, bins in enumerate(lane_bins):
            turns = rows.astype(jnp.float32) * (bins.astype(jnp.float32) * (1.0 / NFFT))
            turns = turns - jnp.round(turns)
            table = cos_turns(turns + quarter) * (1.0 / math.sqrt(NFFT))
            table = table.astype(jnp.bfloat16).astype(jnp.float32)
            flipped = table * jnp.where(bins % 2 == 1, -1.0, 1.0)
            for tile in range(out_tile, columns // LANES, out_tiles):
                lanes = slice(tile * LANES, (tile + 1) * LANES)
                for window, values, factor in zip(windows, (table, flipped), factors):
                    w_ref[window, lanes] = (values * factor[:, lanes]).astype(w_ref.dtype)
        return carry

    lax.fori_loop(0, half // block, some, 0)


def spectra_kernel(chunk, frames, width, signs,
                   bins_ref, basis_ref, mix_ref, minor_mix_ref, samples_ref, out_ref,
                   x_ref, arrived, w_ref, major_ref, minor_ref, acc_ref, turned_ref):
    step = pl.program_id(0)
    steps = pl.num_programs(0)
    signals = samples_ref.shape[0]
    columns = w_ref.shape[1]
    behind = TAPS - 1 + chunk
    pad = behind % chunk
    size = min(width, LANES)
    out_tiles = width // size

    def fetch(at):
        block = x_ref.shape[2]
        return pltpu.make_async_copy(
            samples_ref.at[:, pl.ds(pl.multiple_of(at * block, block), block)],
            x_ref.at[at % 2],
            arrived.at[at % 2],
        )

    @pl.when(step == 0)
    def _():
        fetch(0).start()

    @pl.when(step + 1 < steps)
    def _():
        fetch(step + 1).start()

    @pl.when(step == 0)
    def _():
        fill_weights(bins_ref, basis_ref, w_ref, width, out_tiles)
        major_ref[: behind + pad] = jnp.zeros((behind + pad,) + major_ref.shape[1:], jnp.float32)
        minor_ref[: behind + pad] = jnp.zeros((behind + pad,) + minor_ref.shape[1:], jnp.bfloat16)

    def weigh(totals, held, factors, sign):
        for k in range(TAPS // 2):
            for o in range(len(totals)):
                low, high = held[o + k], held[o + TAPS - 1 - k]
                totals[o] = totals[o] + factors[k] * (low + high if sign > 0 else low - high)

    def combine(slot, begin, count, start):
        first = jnp.maximum(slot * chunk - behind + pad, 0) + begin
        frames_in = count + TAPS - 1
        seen = None
        for out_tile in range(out_tiles):
            small = [jnp.zeros((16, LANES), jnp.bfloat16) for _ in range(count)]
            for tile in range(out_tile, columns // 2 // LANES, out_tiles):
                lanes = slice(tile * LANES, (tile + 1) * LANES)
                held = [minor_ref[first + i, pl.ds(start, 16), lanes] for i in range(frames_in)]
                factors = [minor_mix_ref[tile, k] for k in range(TAPS // 2)]
                weigh(small, held, factors, signs[(columns // 2 // LANES + tile) // out_tiles])
            wide = [total.astype(jnp.float32) for total in small]
            for row in (0, 8):
                window = pl.ds(start + row, 8)
                totals = [total[row : row + 8] for total in wide]
                for tile in range(out_tile, columns // 2 // LANES, out_tiles):
                    lanes = slice(tile * LANES, (tile + 1) * LANES)
                    held = [major_ref[first + i, window, lanes] for i in range(frames_in)]
                    factors = [mix_ref[tile, k : k + 1, :] for k in range(TAPS // 2)]
                    weigh(totals, held, factors, signs[tile // out_tiles])
                for o in range(count):
                    acc_ref[slot * chunk + begin + o, out_tile, window, :] = totals[o]
                    seen = totals[o] if seen is None else seen + totals[o]
        return jnp.maximum(jnp.minimum(seen, 0.0), 0.0)

    groups = -(-chunk // 4)
    bounds = [chunk * i // groups for i in range(groups + 1)]
    shares = [
        (begin, end - begin, start)
        for begin, end in zip(bounds[:-1], bounds[1:])
        for start in range(0, signals, 16)
    ]

    def turn(slot):
        unit = jnp.where(
            lax.broadcasted_iota(jnp.int32, (size, 2 * LANES), 0)
            == lax.broadcasted_iota(jnp.int32, (size, 2 * LANES), 1) % size, 1.0, 0.0
        ).astype(jnp.bfloat16)
        together = chunk if signals % LANES == 0 else 1
        for out_tile in range(out_tiles):
            for at in range(0, chunk, together):
                total = jnp.concatenate(
                    [acc_ref[slot * chunk + at + i, out_tile] for i in range(together)], axis=0
                )
                high = total.astype(jnp.bfloat16)
                low = (total - high.astype(jnp.float32)).astype(jnp.bfloat16)
                both = jnp.concatenate([high, low], axis=1)
                turned = lax.dot_general(unit, both, NT, preferred_element_type=jnp.float32)
                for i in range(together):
                    turned_ref[out_tile * size : (out_tile + 1) * size, slot * chunk + at + i, :] = (
                        turned[:, i * signals : (i + 1) * signals]
                    )

    fetch(step).wait()
    slot = step % 2
    pieces = 16
    depth = NFFT // pieces
    zero = None
    turn(jnp.maximum(step - 1, 0))
    product = None
    for piece in range(pieces):
        parts = [
            x_ref[slot, :, i * NFFT + piece * depth : i * NFFT + (piece + 1) * depth]
            for i in range(chunk)
        ]
        if zero is not None and any(share * pieces // len(shares) == piece for share in range(len(shares))):
            zero = jnp.concatenate([zero, zero], axis=0).astype(jnp.bfloat16)
            top = jnp.concatenate([parts[0][:16, :LANES] + zero, parts[0][:16, LANES:]], axis=1)
            parts[0] = jnp.concatenate([top, parts[0][16:]], axis=0)
            zero = None
        part = jnp.dot(
            jnp.concatenate(parts, axis=0),
            w_ref[piece * depth : (piece + 1) * depth, :],
            preferred_element_type=jnp.float32,
        )
        product = part if product is None else product + part
        for share in range(len(shares)):
            if share * pieces // len(shares) == piece:
                more = combine(step, *shares[share])
                zero = more if zero is None else zero + more
    window = pl.ds(step * chunk + pad, chunk)
    major_ref[window] = product[:, : columns // 2].reshape(chunk, signals, columns // 2)
    minor = product[:, columns // 2 :].astype(jnp.bfloat16)
    minor_ref[window] = minor.reshape(chunk, signals, columns // 2)

    @pl.when(step == steps - 1)
    def _():
        chunks = (frames + TAPS - 1) // chunk
        for share in shares:
            combine(chunks, *share)
        turn(chunks - 1)
        turn(chunks)
        for row in range(width):
            out_ref[row] = turned_ref[row, behind : behind + frames, :].astype(out_ref.dtype)


def spectra_of(samples, chan_bins, frames):
    signals, length = samples.shape
    in_frames = length // NFFT
    width = 2 * chan_bins.shape[0]
    columns = RANK * width
    size = min(width, LANES)
    out_tiles = width // size
    chunk = max(d for d in (1, 3, 7) if in_frames % d == 0)
    behind = TAPS - 1 + chunk
    slots = (in_frames // chunk + 1) * chunk

    mix, basis, parity = taps_factors()
    tiles = term_tiles(parity, LANES // size)
    signs = tuple(sign for _, sign in tiles)
    order = [r for terms, _ in tiles for r in terms]
    lanes = np.repeat(mix[: TAPS // 2, order], width, axis=1).astype(np.float32)
    lanes = lanes.reshape(TAPS // 2, -1, LANES).transpose(1, 0, 2)
    major, minor = np.split(lanes, 2)
    minor = np.repeat(minor[:, :, None, :], 16, axis=2).astype(jnp.bfloat16)
    pieces, left = [], basis[order].T.astype(np.float32)
    for _ in range(3):
        pieces.append(left.astype(jnp.bfloat16))
        left = left - pieces[-1].astype(np.float32)
    pieces.append(np.zeros((NFFT, LANES - 3 * RANK), jnp.bfloat16))

    whole = pl.BlockSpec(memory_space=pltpu.VMEM)
    return pl.pallas_call(
        functools.partial(spectra_kernel, chunk, frames, width, signs),
        grid=(in_frames // chunk,),
        in_specs=[
            pl.BlockSpec(memory_space=pltpu.SMEM), whole, whole, whole,
            pl.BlockSpec(memory_space=pl.ANY),
        ],
        out_specs=pl.BlockSpec((width, frames, signals), lambda i: (0, 0, 0)),
        out_shape=jax.ShapeDtypeStruct((width, frames, signals), jnp.bfloat16),
        scratch_shapes=[
            pltpu.VMEM((2, signals, chunk * NFFT), jnp.bfloat16),
            pltpu.SemaphoreType.DMA((2,)),
            pltpu.VMEM((NFFT, columns), jnp.bfloat16),
            pltpu.VMEM((in_frames + behind % chunk, signals, columns // 2), jnp.float32),
            pltpu.VMEM((in_frames + behind % chunk, signals, columns // 2), jnp.bfloat16),
            pltpu.VMEM((slots, out_tiles, signals, LANES), jnp.float32),
            pltpu.VMEM((width, slots, signals), jnp.float32),
        ],
        compiler_params=pltpu.CompilerParams(vmem_limit_bytes=60 << 20),
        cost_estimate=pl.CostEstimate(
            flops=2 * signals * length * columns,
            bytes_accessed=2 * signals * length,
            transcendentals=0,
        ),
        name="spectra",
    )(chan_bins, jnp.asarray(np.concatenate(pieces, axis=1)), jnp.asarray(major), jnp.asarray(minor), samples)


def steering_kernel(bin_ref, delays_ref, beams_ref, antennas_ref, table_ref, place_ref, raw_ref):
    pointings, antennas = delays_ref.shape
    beams = beams_ref.shape[1]
    rows = 32
    turn = bin_ref[0, 0]

    def some(at, carry):
        window = pl.ds(pl.multiple_of(at * rows, rows), rows)
        turns = delays_ref[window, :] * turn * (1.0 / NFFT)
        raw_ref[window, :antennas] = cos_turns(turns).astype(jnp.bfloat16)
        raw_ref[window, antennas:] = cos_turns(turns - 0.25).astype(jnp.bfloat16)
        return carry

    lax.fori_loop(0, pointings // rows, some, 0)
    column = jnp.broadcast_to(antennas_ref[...], (LANES, antennas)).T
    for tile in range(antennas // LANES):
        lanes = lax.broadcasted_iota(jnp.int32, (antennas, LANES), 1) + tile * LANES
        place_ref[:, tile * LANES : (tile + 1) * LANES] = jnp.where(
            column == lanes, 1.0, 0.0
        ).astype(jnp.bfloat16)
    wanted = jnp.broadcast_to(beams_ref[...], (LANES, beams)).T
    chosen = jnp.concatenate(
        [
            jnp.where(
                wanted == lax.broadcasted_iota(jnp.int32, (beams, LANES), 1) + tile * LANES, 1.0, 0.0
            ).astype(jnp.bfloat16)
            for tile in range(pointings // LANES)
        ],
        axis=1,
    )
    for part in range(2):
        ordered = jnp.dot(
            chosen, raw_ref[:, part * antennas : (part + 1) * antennas],
            preferred_element_type=jnp.float32,
        ).astype(jnp.bfloat16)
        table_ref[part] = jnp.dot(
            ordered, place_ref[...], preferred_element_type=jnp.float32
        ).astype(jnp.bfloat16)


def steering_of(bin_value, delays, beam_index, antenna_map):
    pointings, antennas = delays.shape
    beams = beam_index.shape[0]
    vmem = pl.BlockSpec(memory_space=pltpu.VMEM)
    return pl.pallas_call(
        steering_kernel,
        in_specs=[pl.BlockSpec(memory_space=pltpu.SMEM), vmem, vmem, vmem],
        out_specs=[vmem, vmem],
        out_shape=[
            jax.ShapeDtypeStruct((2, beams, antennas), jnp.bfloat16),
            jax.ShapeDtypeStruct((antennas, antennas), jnp.bfloat16),
        ],
        scratch_shapes=[pltpu.VMEM((pointings, 2 * antennas), jnp.bfloat16)],
        compiler_params=pltpu.CompilerParams(vmem_limit_bytes=32 << 20),
        cost_estimate=pl.CostEstimate(
            flops=40 * pointings * antennas + 4 * beams * antennas * (antennas + pointings),
            bytes_accessed=8 * pointings * antennas,
            transcendentals=0,
        ),
        name="steering",
    )(bin_value.reshape(1, 1), delays, beam_index.reshape(1, beams), antenna_map.reshape(1, antennas))


def series_of(moved):
    if len(moved.shape) == 3:
        real, imag = moved[0], moved[1]
    else:
        blocks, groups = moved.shape[:2]
        real, imag = (
            jnp.concatenate(
                [
                    jnp.concatenate([moved[q, f, part] for f in range(groups)], axis=1)
                    for q in range(blocks)
                ],
                axis=0,
            )
            for part in range(2)
        )
    return jnp.concatenate([real, imag], axis=0), jnp.concatenate([imag, -real], axis=0)


def beams_kernel(scale, moved_ref, table_ref, out_ref):
    straight, crossed = series_of(moved_ref)
    formed = lax.dot_general(table_ref[0], straight, NT, preferred_element_type=jnp.float32)
    formed += lax.dot_general(table_ref[1], crossed, NT, preferred_element_type=jnp.float32)
    formed = (formed * scale).astype(out_ref.dtype)
    out_ref[...] = formed.reshape(out_ref.shape)


def beams_of(moved, table, groups, times):
    _, beams, antennas = table.shape
    vmem = pl.BlockSpec(memory_space=pltpu.VMEM)
    return pl.pallas_call(
        functools.partial(beams_kernel, 1.0 / math.sqrt(antennas)),
        in_specs=[vmem, vmem],
        out_specs=vmem,
        out_shape=jax.ShapeDtypeStruct((groups, beams // groups, 2 * times), jnp.bfloat16),
        compiler_params=pltpu.CompilerParams(vmem_limit_bytes=32 << 20),
        name="beams",
    )(moved, table)


def visibility_kernel(moved_ref, place_ref, out_ref, straight_ref, crossed_ref):
    step = pl.program_id(0)
    rows = out_ref.shape[2]
    times = straight_ref.shape[1] // 2

    @pl.when(step == 0)
    def _():
        for wide, held in zip(series_of(moved_ref), (straight_ref, crossed_ref)):
            held[...] = lax.dot_general(
                place_ref[...], wide, NT, preferred_element_type=jnp.float32
            ).astype(jnp.bfloat16)

    window = pl.ds(pl.multiple_of(step * rows, rows), rows)
    for part, held in enumerate((straight_ref, crossed_ref)):
        out_ref[0, part] = lax.dot_general(
            held[window, :], straight_ref[...], NT, preferred_element_type=jnp.float32
        ) * (1.0 / times)


def visibilities_of(moved, place, times):
    antennas = place.shape[0]
    rows = antennas // 4
    return pl.pallas_call(
        visibility_kernel,
        grid=(antennas // rows,),
        in_specs=[
            pl.BlockSpec(moved.shape, lambda i: (0,) * len(moved.shape)),
            pl.BlockSpec(place.shape, lambda i: (0, 0)),
        ],
        out_specs=pl.BlockSpec((1, 2, rows, antennas), lambda i: (0, 0, i, 0)),
        out_shape=jax.ShapeDtypeStruct((1, 2, antennas, antennas), jnp.float32),
        scratch_shapes=[pltpu.VMEM((antennas, 2 * times), jnp.bfloat16)] * 2,
        compiler_params=pltpu.CompilerParams(vmem_limit_bytes=32 << 20),
        cost_estimate=pl.CostEstimate(
            flops=8 * antennas * antennas * 2 * times,
            bytes_accessed=8 * antennas * antennas,
            transcendentals=0,
        ),
        name="visibilities",
    )(moved, place)


def body(voltages, chan_bins, antenna_map, beam_index, delays):
    signals_dev = voltages.shape[1]
    frames = voltages.shape[2] // NFFT - TAPS + 1
    channels = chan_bins.shape[0]
    tm_count = lax.axis_size("tm")
    freq_count = lax.axis_size("freq")
    times = tm_count * frames

    spectra = spectra_of(voltages[0], chan_bins, frames)
    spectra = spectra.reshape(channels, 2, frames, signals_dev)
    moved = lax.all_to_all(spectra, ("tm", "freq"), split_axis=0, concat_axis=0, tiled=True)
    moved = moved.reshape(tm_count, freq_count, 2, frames, signals_dev)
    if signals_dev % LANES:
        moved = moved.transpose(2, 0, 3, 1, 4).reshape(2, times, freq_count * signals_dev)

    channel = lax.axis_index("tm") * freq_count + lax.axis_index("freq")
    bin_value = lax.dynamic_index_in_dim(chan_bins, channel, keepdims=False)
    table, place = steering_of(bin_value.astype(jnp.float32), delays, beam_index, antenna_map)
    formed = beams_of(moved, table, freq_count, times)
    turned = lax.all_to_all(formed, "freq", split_axis=0, concat_axis=0, tiled=True)
    visibilities = visibilities_of(moved, place, times)
    turned = turned.transpose(1, 0, 2).astype(jnp.float32)
    return (visibilities, turned.reshape(turned.shape[0], turned.shape[1], 2, times))


def solution(mesh):
    return jax.shard_map(
        body,
        mesh=mesh,
        in_specs=(P("tm", "freq", None), P(), P(), P(), P()),
        out_specs=(P(("tm", "freq"), None, None, None), P("freq", "tm", None, None)),
        check_vma=False,
    )
```

```python
import functools
import math

import jax
import jax.numpy as jnp
import numpy as np
from jax import lax
from jax.experimental import pallas as pl
from jax.experimental.pallas import tpu as pltpu
from jax.sharding import PartitionSpec as P

NFFT = 4096
TAPS = 16
RANK = 8
LANES = 128
NT = (((1,), (1,)), ((), ()))


def taps_factors():
    total = TAPS * NFFT
    offsets = np.arange(total, dtype=np.float64)
    shifted = (offsets - 0.5 * total + 0.5) / NFFT
    window = 0.5 - 0.5 * np.cos(2.0 * np.pi / total * (offsets + 0.5))
    taps = (np.sinc(shifted) * window).reshape(TAPS, NFFT)
    left, _, _ = np.linalg.svd(taps, full_matrices=False)
    mix = np.round(left[:, :RANK], 7)
    parity = []
    for r in range(RANK):
        sign = 1.0 if np.sum(mix[:, r] * mix[::-1, r]) > 0 else -1.0
        mix[:, r] = 0.5 * (mix[:, r] + sign * mix[::-1, r])
        parity.append(sign)
    gram = np.sum(mix[:, :, None] * mix[:, None, :], axis=0)
    inverse = np.linalg.inv(gram)
    basis = np.zeros((RANK, NFFT))
    for r in range(RANK):
        dual = np.sum(mix * inverse[r], axis=1)
        basis[r] = np.sum(dual[:, None] * taps, axis=0)
    return mix, basis, parity


def term_tiles(parity, per_tile):
    tiles = []
    for half in (range(RANK // 2), range(RANK // 2, RANK)):
        for wanted in (1.0, -1.0):
            group = [r for r in half if parity[r] == wanted]
            for at in range(0, len(group), per_tile):
                tiles.append((tuple(group[at : at + per_tile]), wanted))
    return tiles


def cos_turns(turns):
    rest = 0.25 - jnp.abs(turns - jnp.round(turns))
    angle = rest * (2.0 * math.pi)
    square = angle * angle
    total = -1.0 / math.factorial(11) + square * (1.0 / math.factorial(13))
    for power in (9, 7, 5, 3):
        total = (-1.0) ** (power // 2) / math.factorial(power) + square * total
    return angle + angle * square * total


def fill_weights(bins_ref, basis_ref, w_ref, width, out_tiles):
    columns = w_ref.shape[1]
    splits = basis_ref.shape[1]
    block = 2 * LANES
    half = NFFT // 2
    source = lax.broadcasted_iota(jnp.int32, (splits, columns), 0)
    term = lax.broadcasted_iota(jnp.int32, (splits, columns), 1) // width
    spread = jnp.where(source % RANK == term, 1.0, 0.0).astype(jnp.bfloat16)
    lane = lax.broadcasted_iota(jnp.int32, (1, LANES), 1)
    quarter = jnp.where(lane % 2 == 1, 0.25, 0.0)
    lane_bins = []
    for out_tile in range(out_tiles):
        channel = (lane + out_tile * LANES) % width // 2
        value = jnp.zeros((1, LANES), jnp.int32)
        for at in range(width // 2):
            value = jnp.where(channel == at, bins_ref[at], value)
        lane_bins.append(value)

    def some(at, carry):
        windows = [pl.ds(pl.multiple_of(at * block + i * half, block), block) for i in range(2)]
        rows = lax.broadcasted_iota(jnp.int32, (block, LANES), 0) + at * block
        factors = [
            jnp.dot(basis_ref[window, :], spread, preferred_element_type=jnp.float32)
            for window in windows
        ]
        for out_tile, bins in enumerate(lane_bins):
            turns = rows.astype(jnp.float32) * (bins.astype(jnp.float32) * (1.0 / NFFT))
            turns = turns - jnp.round(turns)
            table = cos_turns(turns + quarter) * (1.0 / math.sqrt(NFFT))
            table = table.astype(jnp.bfloat16).astype(jnp.float32)
            flipped = table * jnp.where(bins % 2 == 1, -1.0, 1.0)
            for tile in range(out_tile, columns // LANES, out_tiles):
                lanes = slice(tile * LANES, (tile + 1) * LANES)
                for window, values, factor in zip(windows, (table, flipped), factors):
                    w_ref[window, lanes] = (values * factor[:, lanes]).astype(w_ref.dtype)
        return carry

    lax.fori_loop(0, half // block, some, 0)


def spectra_kernel(chunk, frames, width, signs,
                   bins_ref, basis_ref, mix_ref, minor_mix_ref, samples_ref, out_ref,
                   x_ref, arrived, w_ref, major_ref, minor_ref, acc_ref, turned_ref):
    step = pl.program_id(0)
    steps = pl.num_programs(0)
    signals = samples_ref.shape[0]
    columns = w_ref.shape[1]
    behind = TAPS - 1 + chunk
    pad = behind % chunk
    size = min(width, LANES)
    out_tiles = width // size

    def fetch(at):
        block = x_ref.shape[2]
        return pltpu.make_async_copy(
            samples_ref.at[:, pl.ds(pl.multiple_of(at * block, block), block)],
            x_ref.at[at % 2],
            arrived.at[at % 2],
        )

    @pl.when(step == 0)
    def _():
        fetch(0).start()

    @pl.when(step + 1 < steps)
    def _():
        fetch(step + 1).start()

    @pl.when(step == 0)
    def _():
        fill_weights(bins_ref, basis_ref, w_ref, width, out_tiles)
        major_ref[: behind + pad] = jnp.zeros((behind + pad,) + major_ref.shape[1:], jnp.float32)
        minor_ref[: behind + pad] = jnp.zeros((behind + pad,) + minor_ref.shape[1:], jnp.bfloat16)

    def weigh(totals, held, factors, sign):
        for k in range(TAPS // 2):
            for o in range(len(totals)):
                low, high = held[o + k], held[o + TAPS - 1 - k]
                totals[o] = totals[o] + factors[k] * (low + high if sign > 0 else low - high)

    def combine(slot, begin, count, start):
        first = jnp.maximum(slot * chunk - behind + pad, 0) + begin
        frames_in = count + TAPS - 1
        seen = None
        for out_tile in range(out_tiles):
            small = [jnp.zeros((16, LANES), jnp.bfloat16) for _ in range(count)]
            for tile in range(out_tile, columns // 2 // LANES, out_tiles):
                lanes = slice(tile * LANES, (tile + 1) * LANES)
                held = [minor_ref[first + i, pl.ds(start, 16), lanes] for i in range(frames_in)]
                factors = [minor_mix_ref[tile, k] for k in range(TAPS // 2)]
                weigh(small, held, factors, signs[(columns // 2 // LANES + tile) // out_tiles])
            wide = [total.astype(jnp.float32) for total in small]
            for row in (0, 8):
                window = pl.ds(start + row, 8)
                totals = [total[row : row + 8] for total in wide]
                for tile in range(out_tile, columns // 2 // LANES, out_tiles):
                    lanes = slice(tile * LANES, (tile + 1) * LANES)
                    held = [major_ref[first + i, window, lanes] for i in range(frames_in)]
                    factors = [mix_ref[tile, k : k + 1, :] for k in range(TAPS // 2)]
                    weigh(totals, held, factors, signs[tile // out_tiles])
                for o in range(count):
                    acc_ref[slot * chunk + begin + o, out_tile, window, :] = totals[o]
                    seen = totals[o] if seen is None else seen + totals[o]
        return jnp.maximum(jnp.minimum(seen, 0.0), 0.0)

    groups = -(-chunk // 4)
    bounds = [chunk * i // groups for i in range(groups + 1)]
    shares = [
        (begin, end - begin, start)
        for begin, end in zip(bounds[:-1], bounds[1:])
        for start in range(0, signals, 16)
    ]

    def turn(slot):
        unit = jnp.where(
            lax.broadcasted_iota(jnp.int32, (size, 2 * LANES), 0)
            == lax.broadcasted_iota(jnp.int32, (size, 2 * LANES), 1) % size, 1.0, 0.0
        ).astype(jnp.bfloat16)
        together = chunk if signals % LANES == 0 else 1
        for out_tile in range(out_tiles):
            for at in range(0, chunk, together):
                total = jnp.concatenate(
                    [acc_ref[slot * chunk + at + i, out_tile] for i in range(together)], axis=0
                )
                high = total.astype(jnp.bfloat16)
                low = (total - high.astype(jnp.float32)).astype(jnp.bfloat16)
                both = jnp.concatenate([high, low], axis=1)
                turned = lax.dot_general(unit, both, NT, preferred_element_type=jnp.float32)
                for i in range(together):
                    turned_ref[out_tile * size : (out_tile + 1) * size, slot * chunk + at + i, :] = (
                        turned[:, i * signals : (i + 1) * signals]
                    )

    fetch(step).wait()
    slot = step % 2
    pieces = 16
    depth = NFFT // pieces
    zero = None
    turn(jnp.maximum(step - 1, 0))
    product = None
    for piece in range(pieces):
        parts = [
            x_ref[slot, :, i * NFFT + piece * depth : i * NFFT + (piece + 1) * depth]
            for i in range(chunk)
        ]
        if zero is not None and any(share * pieces // len(shares) == piece for share in range(len(shares))):
            zero = jnp.concatenate([zero, zero], axis=0).astype(jnp.bfloat16)
            top = jnp.concatenate([parts[0][:16, :LANES] + zero, parts[0][:16, LANES:]], axis=1)
            parts[0] = jnp.concatenate([top, parts[0][16:]], axis=0)
            zero = None
        part = jnp.dot(
            jnp.concatenate(parts, axis=0),
            w_ref[piece * depth : (piece + 1) * depth, :],
            preferred_element_type=jnp.float32,
        )
        product = part if product is None else product + part
        for share in range(len(shares)):
            if share * pieces // len(shares) == piece:
                more = combine(step, *shares[share])
                zero = more if zero is None else zero + more
    window = pl.ds(step * chunk + pad, chunk)
    major_ref[window] = product[:, : columns // 2].reshape(chunk, signals, columns // 2)
    minor = product[:, columns // 2 :].astype(jnp.bfloat16)
    minor_ref[window] = minor.reshape(chunk, signals, columns // 2)

    @pl.when(step == steps - 1)
    def _():
        chunks = (frames + TAPS - 1) // chunk
        for share in shares:
            combine(chunks, *share)
        turn(chunks - 1)
        turn(chunks)
        for row in range(width):
            out_ref[row] = turned_ref[row, behind : behind + frames, :].astype(out_ref.dtype)


def spectra_of(samples, chan_bins, frames):
    signals, length = samples.shape
    in_frames = length // NFFT
    width = 2 * chan_bins.shape[0]
    columns = RANK * width
    size = min(width, LANES)
    out_tiles = width // size
    chunk = max(d for d in (1, 3, 7) if in_frames % d == 0)
    behind = TAPS - 1 + chunk
    slots = (in_frames // chunk + 1) * chunk

    mix, basis, parity = taps_factors()
    tiles = term_tiles(parity, LANES // size)
    signs = tuple(sign for _, sign in tiles)
    order = [r for terms, _ in tiles for r in terms]
    lanes = np.repeat(mix[: TAPS // 2, order], width, axis=1).astype(np.float32)
    lanes = lanes.reshape(TAPS // 2, -1, LANES).transpose(1, 0, 2)
    major, minor = np.split(lanes, 2)
    minor = np.repeat(minor[:, :, None, :], 16, axis=2).astype(jnp.bfloat16)
    pieces, left = [], basis[order].T.astype(np.float32)
    for _ in range(3):
        pieces.append(left.astype(jnp.bfloat16))
        left = left - pieces[-1].astype(np.float32)
    pieces.append(np.zeros((NFFT, LANES - 3 * RANK), jnp.bfloat16))

    whole = pl.BlockSpec(memory_space=pltpu.VMEM)
    return pl.pallas_call(
        functools.partial(spectra_kernel, chunk, frames, width, signs),
        grid=(in_frames // chunk,),
        in_specs=[
            pl.BlockSpec(memory_space=pltpu.SMEM), whole, whole, whole,
            pl.BlockSpec(memory_space=pl.ANY),
        ],
        out_specs=pl.BlockSpec((width, frames, signals), lambda i: (0, 0, 0)),
        out_shape=jax.ShapeDtypeStruct((width, frames, signals), jnp.bfloat16),
        scratch_shapes=[
            pltpu.VMEM((2, signals, chunk * NFFT), jnp.bfloat16),
            pltpu.SemaphoreType.DMA((2,)),
            pltpu.VMEM((NFFT, columns), jnp.bfloat16),
            pltpu.VMEM((in_frames + behind % chunk, signals, columns // 2), jnp.float32),
            pltpu.VMEM((in_frames + behind % chunk, signals, columns // 2), jnp.bfloat16),
            pltpu.VMEM((slots, out_tiles, signals, LANES), jnp.float32),
            pltpu.VMEM((width, slots, signals), jnp.float32),
        ],
        compiler_params=pltpu.CompilerParams(vmem_limit_bytes=60 << 20),
        cost_estimate=pl.CostEstimate(
            flops=2 * signals * length * columns,
            bytes_accessed=2 * signals * length,
            transcendentals=0,
        ),
        name="spectra",
    )(chan_bins, jnp.asarray(np.concatenate(pieces, axis=1)), jnp.asarray(major), jnp.asarray(minor), samples)


def steering_kernel(bin_ref, delays_ref, beams_ref, antennas_ref, table_ref, place_ref, raw_ref):
    pointings, antennas = delays_ref.shape
    beams = beams_ref.shape[1]
    rows = 32
    turn = bin_ref[0, 0]

    def some(at, carry):
        window = pl.ds(pl.multiple_of(at * rows, rows), rows)
        turns = delays_ref[window, :] * turn * (1.0 / NFFT)
        raw_ref[window, :antennas] = cos_turns(turns).astype(jnp.bfloat16)
        raw_ref[window, antennas:] = cos_turns(turns - 0.25).astype(jnp.bfloat16)
        return carry

    lax.fori_loop(0, pointings // rows, some, 0)
    column = jnp.broadcast_to(antennas_ref[...], (LANES, antennas)).T
    for tile in range(antennas // LANES):
        lanes = lax.broadcasted_iota(jnp.int32, (antennas, LANES), 1) + tile * LANES
        place_ref[:, tile * LANES : (tile + 1) * LANES] = jnp.where(
            column == lanes, 1.0, 0.0
        ).astype(jnp.bfloat16)
    wanted = jnp.broadcast_to(beams_ref[...], (LANES, beams)).T
    chosen = jnp.concatenate(
        [
            jnp.where(
                wanted == lax.broadcasted_iota(jnp.int32, (beams, LANES), 1) + tile * LANES, 1.0, 0.0
            ).astype(jnp.bfloat16)
            for tile in range(pointings // LANES)
        ],
        axis=1,
    )
    for part in range(2):
        ordered = jnp.dot(
            chosen, raw_ref[:, part * antennas : (part + 1) * antennas],
            preferred_element_type=jnp.float32,
        ).astype(jnp.bfloat16)
        table_ref[part] = jnp.dot(
            ordered, place_ref[...], preferred_element_type=jnp.float32
        ).astype(jnp.bfloat16)


def steering_of(bin_value, delays, beam_index, antenna_map):
    pointings, antennas = delays.shape
    beams = beam_index.shape[0]
    vmem = pl.BlockSpec(memory_space=pltpu.VMEM)
    return pl.pallas_call(
        steering_kernel,
        in_specs=[pl.BlockSpec(memory_space=pltpu.SMEM), vmem, vmem, vmem],
        out_specs=[vmem, vmem],
        out_shape=[
            jax.ShapeDtypeStruct((2, beams, antennas), jnp.bfloat16),
            jax.ShapeDtypeStruct((antennas, antennas), jnp.bfloat16),
        ],
        scratch_shapes=[pltpu.VMEM((pointings, 2 * antennas), jnp.bfloat16)],
        compiler_params=pltpu.CompilerParams(vmem_limit_bytes=32 << 20),
        cost_estimate=pl.CostEstimate(
            flops=40 * pointings * antennas + 4 * beams * antennas * (antennas + pointings),
            bytes_accessed=8 * pointings * antennas,
            transcendentals=0,
        ),
        name="steering",
    )(bin_value.reshape(1, 1), delays, beam_index.reshape(1, beams), antenna_map.reshape(1, antennas))


def series_of(moved):
    if len(moved.shape) == 3:
        real, imag = moved[0], moved[1]
    else:
        blocks, groups = moved.shape[:2]
        real, imag = (
            jnp.concatenate(
                [
                    jnp.concatenate([moved[q, f, part] for f in range(groups)], axis=1)
                    for q in range(blocks)
                ],
                axis=0,
            )
            for part in range(2)
        )
    return jnp.concatenate([real, imag], axis=0), jnp.concatenate([imag, -real], axis=0)


def beams_kernel(scale, moved_ref, table_ref, out_ref):
    straight, crossed = series_of(moved_ref)
    formed = lax.dot_general(table_ref[0], straight, NT, preferred_element_type=jnp.float32)
    formed += lax.dot_general(table_ref[1], crossed, NT, preferred_element_type=jnp.float32)
    formed = (formed * scale).astype(out_ref.dtype)
    out_ref[...] = formed.reshape(out_ref.shape)


def beams_of(moved, table, groups, times):
    _, beams, antennas = table.shape
    vmem = pl.BlockSpec(memory_space=pltpu.VMEM)
    return pl.pallas_call(
        functools.partial(beams_kernel, 1.0 / math.sqrt(antennas)),
        in_specs=[vmem, vmem],
        out_specs=vmem,
        out_shape=jax.ShapeDtypeStruct((groups, beams // groups, 2 * times), jnp.bfloat16),
        compiler_params=pltpu.CompilerParams(vmem_limit_bytes=32 << 20),
        name="beams",
    )(moved, table)


def visibility_kernel(moved_ref, place_ref, out_ref, straight_ref, crossed_ref):
    step = pl.program_id(0)
    rows = out_ref.shape[2]
    times = straight_ref.shape[1] // 2

    @pl.when(step == 0)
    def _():
        for wide, held in zip(series_of(moved_ref), (straight_ref, crossed_ref)):
            held[...] = lax.dot_general(
                place_ref[...], wide, NT, preferred_element_type=jnp.float32
            ).astype(jnp.bfloat16)

    window = pl.ds(pl.multiple_of(step * rows, rows), rows)
    for part, held in enumerate((straight_ref, crossed_ref)):
        out_ref[0, part] = lax.dot_general(
            held[window, :], straight_ref[...], NT, preferred_element_type=jnp.float32
        ) * (1.0 / times)


def visibilities_of(moved, place, times):
    antennas = place.shape[0]
    rows = antennas // 4
    return pl.pallas_call(
        visibility_kernel,
        grid=(antennas // rows,),
        in_specs=[
            pl.BlockSpec(moved.shape, lambda i: (0,) * len(moved.shape)),
            pl.BlockSpec(place.shape, lambda i: (0, 0)),
        ],
        out_specs=pl.BlockSpec((1, 2, rows, antennas), lambda i: (0, 0, i, 0)),
        out_shape=jax.ShapeDtypeStruct((1, 2, antennas, antennas), jnp.float32),
        scratch_shapes=[pltpu.VMEM((antennas, 2 * times), jnp.bfloat16)] * 2,
        compiler_params=pltpu.CompilerParams(vmem_limit_bytes=32 << 20),
        cost_estimate=pl.CostEstimate(
            flops=8 * antennas * antennas * 2 * times,
            bytes_accessed=8 * antennas * antennas,
            transcendentals=0,
        ),
        name="visibilities",
    )(moved, place)


def place_kernel(turned_ref, out_ref):
    times = out_ref.shape[3]
    for channel in range(out_ref.shape[1]):
        values = turned_ref[channel].astype(jnp.float32)
        for part in range(2):
            out_ref[:, channel, part, :] = values[:, part * times : (part + 1) * times]


def placed_beams(turned, times):
    channels, beams, _ = turned.shape
    vmem = pl.BlockSpec(memory_space=pltpu.VMEM)
    return pl.pallas_call(
        place_kernel,
        in_specs=[vmem],
        out_specs=vmem,
        out_shape=jax.ShapeDtypeStruct((beams, channels, 2, times), jnp.float32),
        compiler_params=pltpu.CompilerParams(vmem_limit_bytes=32 << 20),
        name="place_beams",
    )(turned)


def body(voltages, chan_bins, antenna_map, beam_index, delays):
    signals_dev = voltages.shape[1]
    frames = voltages.shape[2] // NFFT - TAPS + 1
    channels = chan_bins.shape[0]
    tm_count = lax.axis_size("tm")
    freq_count = lax.axis_size("freq")
    times = tm_count * frames

    spectra = spectra_of(voltages[0], chan_bins, frames)
    spectra = spectra.reshape(channels, 2, frames, signals_dev)
    moved = lax.all_to_all(spectra, ("tm", "freq"), split_axis=0, concat_axis=0, tiled=True)
    moved = moved.reshape(tm_count, freq_count, 2, frames, signals_dev)
    if signals_dev % LANES:
        moved = moved.transpose(2, 0, 3, 1, 4).reshape(2, times, freq_count * signals_dev)

    channel = lax.axis_index("tm") * freq_count + lax.axis_index("freq")
    bin_value = lax.dynamic_index_in_dim(chan_bins, channel, keepdims=False)
    table, place = steering_of(bin_value.astype(jnp.float32), delays, beam_index, antenna_map)
    formed = beams_of(moved, table, freq_count, times)
    turned = lax.all_to_all(formed, "freq", split_axis=0, concat_axis=0, tiled=True)
    visibilities = visibilities_of(moved, place, times)
    return (visibilities, placed_beams(turned, times))


def solution(mesh):
    return jax.shard_map(
        body,
        mesh=mesh,
        in_specs=(P("tm", "freq", None), P(), P(), P(), P()),
        out_specs=(P(("tm", "freq"), None, None, None), P("freq", "tm", None, None)),
        check_vma=False,
    )
```
